256 devices in a mesh: dp: 8 (over z), ctx: 16 (over x, y_hi, core), kvh: 2 (over y_lo).
Axes of the slice: x: 4, y: 4 (y_hi: 2, y_lo: 2; y = y_hi * 2 + y_lo), z: 8, core: 2. Of those that a mesh axis runs over, the one named last changes fastest.
Arguments:
- query_heads: bfloat16 [16384, 1792], P(('dp', 'ctx', 'kvh')), may hold values from -210 to 210
- key_heads: bfloat16 [16384, 256], P(('dp', 'ctx', 'kvh')), may hold values from -7 to 7
- pool_values: bfloat16 [16384, 256], P(('dp', 'ctx', 'kvh')), may hold values from -6 to 6
- output_grad: bfloat16 [16384, 1792], P(('dp', 'ctx', 'kvh')), may hold values from -6 to 6
- lengths: int32 [8, 4], replicated, may hold values from 1 to 1024, 2048 in all within a row
- placement: int32 [16384], P(('dp', 'ctx')), may hold values from 0 to 15, as said below
Outputs:
- attended: bfloat16 [32768, 1792], P(('dp', 'ctx'), 'kvh')
- grad_query: bfloat16 [32768, 1792], P(('dp', 'ctx'), 'kvh')
- key_gradient: bfloat16 [32768, 256], P(('dp', 'ctx'), 'kvh')
- value_gradient: bfloat16 [32768, 256], P(('dp', 'ctx'), 'kvh')
The draws below stay inside these ranges and needn't reach their ends.
Inputs may be any that keep to these rules, and one draw needn't show every extreme that they name: `placement`: of the 128 rows of one pool block, at most 16 have one destination; in every group one destination receives exactly 16 rows from every block of the group, so that one trainer device of each group receives 256 rows.
All inputs are finite; a program needn't handle non-finite values.
Results may differ from the reference program's by a relative error of at most 0.034.
Values may be sent and summed in bfloat16 or wider, within the bound.
No kernel may reach another device: no remote copies, remote signals or barrier semaphores. Data moves between devices by JAX's collectives and lax.ppermute only.
A program may use at most 128 MiB of HBM per device.

```python
import math
import jax
import jax.numpy as jnp
import numpy as np
from jax import lax

QUERY_HEADS = 14
KEY_VALUE_HEADS = 2
HEAD_DIMENSION = 128
ROLL_GRP = 4
TOK_DEV = 128
GROUP_TOKENS = 2048
CAP = 16
SLOTS = 256
POOL_TOKEN_ROWS = 16384
TRAIN_ROWS = 32768
N_DP = 8
N_CTX = 16


def shared_keys(key):
    normal_samples = jax.random.normal(key, (POOL_TOKEN_ROWS, KEY_VALUE_HEADS, HEAD_DIMENSION), jnp.float32)
    random_offset = jax.random.normal(jax.random.fold_in(key, 97), (POOL_TOKEN_ROWS, KEY_VALUE_HEADS, HEAD_DIMENSION), jnp.float32)
    paired = (jnp.arange(POOL_TOKEN_ROWS) % 16 == 5)[:, None, None]
    mixed = random_offset
    return jnp.clip(jnp.where(paired, mixed, normal_samples), -7.0, 7.0)


def draw_key_heads(key, part):
    shared_amount = shared_keys(key)
    return shared_amount.reshape(POOL_TOKEN_ROWS, KEY_VALUE_HEADS * HEAD_DIMENSION).astype(jnp.bfloat16)


def draw_query_heads(key, part):
    key = jax.random.fold_in(key, 5)
    rough_key = jax.random.fold_in(key, 0)
    result = jnp.clip(jax.random.normal(rough_key, (POOL_TOKEN_ROWS, QUERY_HEADS, HEAD_DIMENSION), jnp.float32), -6.0, 6.0)
    return result.reshape(POOL_TOKEN_ROWS, QUERY_HEADS * HEAD_DIMENSION).astype(jnp.bfloat16)


def draw_placement(key, part):
    key = jax.random.fold_in(key, 7)
    busy_key, order_key = jax.random.split(key)
    busy_of_group = jax.random.randint(busy_key, (N_DP,), 0, N_CTX).astype(jnp.int32)
    block_ids = jnp.arange(N_DP * N_CTX, dtype=jnp.int32)
    block_group = (block_ids // N_CTX + block_ids % N_CTX) % N_DP
    busy_block = busy_of_group[block_group]
    block_keys = jax.random.split(order_key, N_DP * N_CTX)

    def one_block(block_key, busy):
        pick_key, shuffle_key = jax.random.split(block_key)
        others = jnp.repeat(jnp.arange(N_CTX - 1, dtype=jnp.int32), CAP)
        others = others + (others >= busy).astype(jnp.int32)
        picked = jax.random.permutation(pick_key, others)[:TOK_DEV - CAP]
        filled = jnp.concatenate([jnp.full((CAP,), busy, jnp.int32), picked])
        return jax.random.permutation(shuffle_key, filled)
    return jax.vmap(one_block)(block_keys, busy_block).reshape(-1).astype(jnp.int32)


def block_scale(rng, dims, shards, low, high):
    def one(dim, parts):
        steps = jax.random.uniform(jax.random.fold_in(jax.random.fold_in(rng, 6), dim), (parts,), jnp.float32, low / len(shards), high / len(shards))
        return jnp.repeat(jnp.exp(steps), dims[dim] // parts).reshape((-1,) + (1,) * (len(dims) - dim - 1))

    factor_of = one(*shards[0])
    for cut in shards[1:]:
        factor_of = factor_of * one(*cut)
    return factor_of


def profile(count, total, reach, slope):
    portions = [(1 << 20) // math.isqrt(grade ** slope) + 1 for grade in range(2, count + 1)]
    surplus, given = total - reach - (count - 1), [1] * (count - 1)
    while surplus > 0:
        movable = [i for i in range(count - 1) if given[i] < reach]
        whole, left = sum([portions[i] for i in movable]), surplus
        for i in movable:
            addition = min(reach - given[i], max(1, left * portions[i] // whole), surplus)
            given[i] = given[i] + addition
            surplus = surplus - addition
    return np.array([reach] + given)


def uneven(stream_key, count, total, most, skew):
    if count == 2:
        one = jax.random.randint(stream_key, (), max(1, total - most), min(most, total - 1) + 1)
        return jnp.stack([one, total - one])
    sizes = jnp.asarray(profile(count, total, most, skew), jnp.int32)
    twos = (count - 1) // 2
    source_of, sink = sizes[1:1 + 2 * twos:2], sizes[2:2 + 2 * twos:2]
    room = jnp.minimum(source_of - 1, most - sink)
    moved = jax.random.randint(jax.random.fold_in(stream_key, 1), (twos,), 0, 1 << 20) % (room + 1)
    sizes = sizes.at[1:1 + 2 * twos:2].set(source_of - moved).at[2:2 + 2 * twos:2].set(sink + moved)
    return sizes[jax.random.permutation(jax.random.fold_in(stream_key, 2), count)]


def noise(own_key, shape, deviation, bound, shards=(), kind=jnp.bfloat16):
    values = jax.random.normal(own_key, shape, jnp.float32) * deviation
    if len(shards) > 0:
        values = block_scale(own_key, shape, shards, -0.22, 0.18) * values
    return jnp.clip(values, min=-bound, max=bound).astype(kind)


def setup_inputs(seed: int = 0) -> dict:
    keys = jax.random.split(jax.random.key(seed), 7)
    return {
        "query_heads": draw_query_heads(jax.random.fold_in(keys[6], 71), 0),
        "key_heads": draw_key_heads(jax.random.fold_in(keys[6], 71), 0),
        "pool_values": noise(keys[2], (POOL_TOKEN_ROWS, KEY_VALUE_HEADS * HEAD_DIMENSION), 1.0, 6.0, ((0, 256),)),
        "output_grad": noise(keys[3], (POOL_TOKEN_ROWS, QUERY_HEADS * HEAD_DIMENSION), 1.0, 6.0, ((0, 256),)),
        "lengths": jax.vmap(lambda own: uneven(own, ROLL_GRP, GROUP_TOKENS, GROUP_TOKENS // 2, 2))(jax.random.split(keys[4], N_DP)).reshape((N_DP, ROLL_GRP)).astype(jnp.int32),
        "placement": draw_placement(jax.random.fold_in(keys[6], 71), 0),
    }


MASKED_LOGIT = -1e+30

def head_pass(query_head, key_head, value_head, grad_head, visible, scaling):
    logits = jnp.dot(query_head, key_head.T, preferred_element_type=jnp.float32) * scaling
    row_top = lax.optimization_barrier(jnp.max(jnp.where(visible, logits, MASKED_LOGIT), axis=1))
    expo = jnp.where(visible, jnp.exp(logits - row_top[:, None]), 0.0)
    row_total = lax.optimization_barrier(jnp.sum(expo, axis=1))
    probs = expo.astype(jnp.bfloat16)
    attended = (jnp.dot(probs, value_head, preferred_element_type=jnp.float32) / row_total[:, None]).astype(jnp.bfloat16)
    lse = row_top + jnp.log(row_total)
    weights = jnp.where(visible, jnp.exp(logits - lse[:, None]), 0.0)
    value_gradient = jnp.dot(weights.astype(jnp.bfloat16).T, grad_head, preferred_element_type=jnp.float32)
    dprob = jnp.dot(grad_head, value_head.T, preferred_element_type=jnp.float32)
    attended_wide = lax.optimization_barrier(attended).astype(jnp.float32)
    delta = lax.optimization_barrier(jnp.sum(grad_head.astype(jnp.float32) * attended_wide, axis=1))
    dlogits = (weights * (dprob - delta[:, None])).astype(jnp.bfloat16)
    grad_query = (jnp.dot(dlogits, key_head, preferred_element_type=jnp.float32) * scaling).astype(jnp.bfloat16)
    key_gradient = jnp.dot(dlogits.T, query_head, preferred_element_type=jnp.float32) * scaling
    return (attended, grad_query, key_gradient, value_gradient)

def group_pass(trainer_group, query_heads, key_heads, pool_values, output_grad, lengths):
    ctx_ids = jnp.arange(N_CTX, dtype=jnp.int32)
    block_ids = (trainer_group - ctx_ids) % N_DP * N_CTX + ctx_ids
    row_ids = (block_ids[:, None] * TOK_DEV + jnp.arange(TOK_DEV, dtype=jnp.int32)[None, :]).reshape(-1)
    queries = query_heads[row_ids]
    keys_here = key_heads[row_ids]
    values_here = pool_values[row_ids]
    grads_here = output_grad[row_ids]
    position = jnp.arange(GROUP_TOKENS, dtype=jnp.int32)
    rollout_len = lengths[trainer_group].astype(jnp.int32)
    rollout_end = jnp.cumsum(rollout_len).astype(jnp.int32)
    begins = rollout_end - rollout_len
    inside = (position[:, None] >= begins[None, :]) & (position[:, None] < rollout_end[None, :])
    starts = lax.optimization_barrier(jnp.sum(jnp.where(inside, begins[None, :], 0), axis=1)).astype(jnp.int32)
    visible = (starts[:, None] == starts[None, :]) & (position[None, :] <= position[:, None])
    queries_per_group = QUERY_HEADS // KEY_VALUE_HEADS
    scaling = 1.0 / math.sqrt(HEAD_DIMENSION)

    def per_head(head_id):
        kv_id = head_id // queries_per_group
        query_head = lax.dynamic_slice_in_dim(queries, head_id * HEAD_DIMENSION, HEAD_DIMENSION, 1)
        grad_head = lax.dynamic_slice_in_dim(grads_here, head_id * HEAD_DIMENSION, HEAD_DIMENSION, 1)
        key_head = lax.dynamic_slice_in_dim(keys_here, kv_id * HEAD_DIMENSION, HEAD_DIMENSION, 1)
        value_head = lax.dynamic_slice_in_dim(values_here, kv_id * HEAD_DIMENSION, HEAD_DIMENSION, 1)
        return head_pass(query_head, key_head, value_head, grad_head, visible, scaling)
    attended, grad_query, key_gradient, value_gradient = lax.map(per_head, jnp.arange(QUERY_HEADS, dtype=jnp.int32))
    attended = attended.transpose(1, 0, 2).reshape(GROUP_TOKENS, QUERY_HEADS * HEAD_DIMENSION)
    grad_query = grad_query.transpose(1, 0, 2).reshape(GROUP_TOKENS, QUERY_HEADS * HEAD_DIMENSION)
    key_gradient = key_gradient.reshape(KEY_VALUE_HEADS, queries_per_group, GROUP_TOKENS, HEAD_DIMENSION).sum(axis=1)
    key_gradient = key_gradient.transpose(1, 0, 2).reshape(GROUP_TOKENS, KEY_VALUE_HEADS * HEAD_DIMENSION).astype(jnp.bfloat16)
    value_gradient = value_gradient.reshape(KEY_VALUE_HEADS, queries_per_group, GROUP_TOKENS, HEAD_DIMENSION).sum(axis=1)
    value_gradient = value_gradient.transpose(1, 0, 2).reshape(GROUP_TOKENS, KEY_VALUE_HEADS * HEAD_DIMENSION).astype(jnp.bfloat16)
    return (row_ids, attended, grad_query, key_gradient, value_gradient)

def reference(query_heads, key_heads, pool_values, output_grad, lengths, placement):

    def one_group(trainer_group):
        return group_pass(trainer_group, query_heads, key_heads, pool_values, output_grad, lengths)
    row_ids, attended, grad_query, key_gradient, value_gradient = lax.map(one_group, jnp.arange(N_DP, dtype=jnp.int32))
    flat_rows = row_ids.reshape(-1)
    block_count = N_DP * N_CTX
    destination = placement.reshape(block_count, TOK_DEV).astype(jnp.int32)
    onehot = (destination[:, :, None] == jnp.arange(N_CTX, dtype=jnp.int32)[None, None, :]).astype(jnp.int32)
    earlier = lax.optimization_barrier(jnp.sum((jnp.cumsum(onehot, axis=1).astype(jnp.int32) - onehot) * onehot, axis=2)).astype(jnp.int32)
    block_ids = jnp.arange(block_count, dtype=jnp.int32)
    pool_dp = block_ids // N_CTX
    pool_ctx = block_ids % N_CTX
    trainer_group = (pool_dp + pool_ctx) % N_DP
    target = ((trainer_group[:, None] * N_CTX + destination) * SLOTS + pool_ctx[:, None] * CAP + earlier).reshape(-1)

    def to_slots(member):
        width = member.shape[-1]
        pooled = jnp.zeros((POOL_TOKEN_ROWS, width), member.dtype).at[flat_rows].set(member.reshape(-1, width))
        return jnp.zeros((TRAIN_ROWS, width), member.dtype).at[target].set(pooled)
    return (to_slots(attended), to_slots(grad_query), to_slots(key_gradient), to_slots(value_gradient))
```

```python
import math

import jax
import jax.numpy as jnp
from jax import lax
from jax.experimental import pallas as pl
from jax.experimental.pallas import tpu as pltpu
from jax.sharding import PartitionSpec as P

HEAD = 128
BLOCK = 128
WINDOW = 9
CHUNK = 9
GROUP = 7
OWN = 5
PLACE_ROWS = 8
AXES = ("dp", "ctx", "kvh")
MASKED_LOGIT = -1e30


def dot_nt(a, b):
    return lax.dot_general(a, b, (((1,), (1,)), ((), ())), preferred_element_type=jnp.float32)


def dot_nn(a, b):
    return jnp.dot(a, b, preferred_element_type=jnp.float32)


def slots_of(place):
    lanes = lax.broadcasted_iota(jnp.int32, (BLOCK, BLOCK), 1)
    subs = lax.broadcasted_iota(jnp.int32, (BLOCK, BLOCK), 0)
    earlier = jnp.where(subs < lanes, 1.0, 0.0).astype(jnp.bfloat16)
    hits = [jnp.where(place == float(e), 1.0, 0.0) for e in range(16)]
    counts = dot_nn(jnp.concatenate(hits, axis=0).astype(jnp.bfloat16), earlier)
    slot = place * 16.0
    for e in range(16):
        slot = slot + hits[e] * counts[e * 16:(e + 1) * 16, :]
    return slot


def one_hot_slots(slot):
    slots = lax.broadcasted_iota(jnp.int32, (256, BLOCK), 0).astype(jnp.float32)
    return jnp.where(slot == slots, 1.0, 0.0).astype(jnp.bfloat16)


def attention_kernel(lengths, place, qd_a, qd_b, kv_own, kv_twin, sent, own_grad, twin_grad, box, k_all, v_all, q_all, g_all, w_all, s_all, logit, expo):
    heads = qd_a.shape[1] // (2 * HEAD)
    width = heads * HEAD
    half_rows = BLOCK // 2
    scaling = 1.0 / math.sqrt(HEAD)
    exponent = scaling * math.log2(math.e)
    group, ctx_pos, kvh_pos = (lax.axis_index(name) for name in AXES)
    off = kvh_pos * half_rows
    begin1 = lengths[0, group]
    begin2 = begin1 + lengths[1, group]
    begin3 = begin2 + lengths[2, group]
    lane = lax.broadcasted_iota(jnp.int32, (1, BLOCK), 1)
    position = ctx_pos * BLOCK + (lane ^ off)
    start = jnp.where(
        position >= begin3,
        begin3,
        jnp.where(position >= begin2, begin2, jnp.where(position >= begin1, begin1, 0)),
    )
    first = (ctx_pos - (WINDOW - 1)) * BLOCK
    row = lax.broadcasted_iota(jnp.int32, (BLOCK, BLOCK), 0)
    for t in range(WINDOW):
        block = jnp.maximum(ctx_pos - (WINDOW - 1) + t, 0)
        kv = kv_own if t % 2 == 0 else kv_twin
        for part in range(2):
            rows = slice(t * BLOCK + part * half_rows, t * BLOCK + (part + 1) * half_rows)
            k_all[rows, :] = kv[2 * (block // 2) + part, 0:half_rows, 0:HEAD]
            v_all[rows, :] = kv[2 * (block // 2) + part, 0:half_rows, HEAD:2 * HEAD]
    box[...] = slots_of(place[...])
    own = box[pl.ds(ctx_pos // 2, 1), :]
    own = jnp.where(off == 0, own, jnp.concatenate([own[:, half_rows:], own[:, :half_rows]], axis=1))
    slots = one_hot_slots(own)
    key_t = k_all[...].T
    value_t = v_all[...].T
    for h in range(heads):
        cols = slice(h * HEAD, (h + 1) * HEAD)
        gcols = slice(width + h * HEAD, width + (h + 1) * HEAD)
        q_all[cols, :] = jnp.concatenate([qd_a[:, cols], qd_b[:, cols]], axis=0)
        g_all[cols, :] = jnp.concatenate([qd_a[:, gcols], qd_b[:, gcols]], axis=0)

    def folded(x, op):
        x = x.reshape(x.shape[0] // 8, 8, x.shape[1])
        out = x[0]
        for i in range(1, x.shape[0]):
            out = op(out, x[i])
        return out

    span = CHUNK * BLOCK
    chunk_at = [slice(t * span, (t + 1) * span) for t in range(WINDOW // CHUNK)]
    wide = lax.broadcasted_iota(jnp.int32, (span, BLOCK), 0)
    for h in range(0, heads, GROUP):
        n = min(GROUP, heads - h)
        cols = slice(h * HEAD, (h + n) * HEAD)
        q, g = q_all[cols, :], g_all[cols, :]
        top = None
        for t, rows in enumerate(chunk_at):
            x = dot_nt(k_all[rows, :], q)
            base = first + t * span
            visible = wide >= start - base
            if t == len(chunk_at) - 1:
                visible = visible & (wide <= position - base)
            x = jnp.where(jnp.concatenate([visible] * n, axis=1), x, MASKED_LOGIT)
            logit[rows, :n * HEAD] = x
            x = folded(x, jnp.maximum)
            top = x if top is None else jnp.maximum(top, x)
        top = jnp.max(top, axis=0, keepdims=True)
        total = None
        for t, rows in enumerate(chunk_at):
            x = jnp.exp2((logit[rows, :n * HEAD] - top) * exponent)
            expo[rows, :n * HEAD] = x
            x = folded(x, jnp.add)
            total = x if total is None else total + x
        inverse = 1.0 / jnp.sum(total, axis=0, keepdims=True)
        for t, rows in enumerate(chunk_at):
            w_all[rows, cols] = (expo[rows, :n * HEAD] * inverse).astype(jnp.bfloat16)
        out_b = dot_nn(value_t, w_all[:, cols]).astype(jnp.bfloat16)
        stacked = jnp.concatenate([out_b[:, i * HEAD:(i + 1) * HEAD] for i in range(n)], axis=0)
        sent[:, cols] = dot_nt(slots, stacked).astype(jnp.bfloat16)
        g_t = g.astype(jnp.float32).T
        delta = jnp.sum(g_t * out_b.astype(jnp.float32), axis=0, keepdims=True)
        for t, rows in enumerate(chunk_at):
            dprob = dot_nt(v_all[rows, :], g)
            s_all[rows, cols] = ((expo[rows, :n * HEAD] * inverse) * (dprob - delta)).astype(jnp.bfloat16)
        dq_b = (dot_nn(key_t, s_all[:, cols]) * scaling).astype(jnp.bfloat16)
        stacked = jnp.concatenate([dq_b[:, i * HEAD:(i + 1) * HEAD] for i in range(n)], axis=0)
        sent[:, width + h * HEAD:width + (h + n) * HEAD] = dot_nt(slots, stacked).astype(jnp.bfloat16)
    q_rows = q_all[...]
    g_rows = g_all[...]
    grad_k = dot_nn(s_all[...], q_rows) * scaling
    grad_v = dot_nn(w_all[...], g_rows)
    for t in range(WINDOW):
        rows = slice(t * BLOCK, (t + 1) * BLOCK)
        step = WINDOW - 1 - t
        out = twin_grad if step % 2 else own_grad
        at = slice(step // 2 * BLOCK, (step // 2 + 1) * BLOCK)
        out[at, :HEAD] = grad_k[rows, :].astype(out.dtype)
        out[at, HEAD:] = grad_v[rows, :].astype(out.dtype)


def slots_kernel(box, rows_sent, own_grad, twin_grad, sent):
    ctx_pos = lax.axis_index(AXES[1])
    odd = ctx_pos % 2 == 1
    width = rows_sent.shape[1]
    sent[:, :width] = rows_sent[...]
    for i in range(OWN):
        total = own_grad[i * BLOCK:(i + 1) * BLOCK, :]
        zero = jnp.zeros(total.shape, jnp.float32)
        later = twin_grad[(i - 1) * BLOCK:i * BLOCK, :].astype(jnp.float32) if i > 0 else zero
        level = twin_grad[i * BLOCK:(i + 1) * BLOCK, :].astype(jnp.float32) if i < OWN - 1 else zero
        total = total + jnp.where(odd, later, level)
        block = jnp.maximum(ctx_pos - 2 * i, 0)
        hot = one_hot_slots(box[pl.ds(block // 2, 1), :])
        at = width + i * 2 * HEAD
        sent[:, at:at + 2 * HEAD] = dot_nn(hot, total.astype(jnp.bfloat16)).astype(jnp.bfloat16)


def landing_kernel(got, attended, grad_query, key_gradient, value_gradient):
    width = attended.shape[1]
    rows = got.shape[0]
    attended[...] = got[:, :width]
    grad_query[...] = got[:, width:2 * width]
    for b in range(16):
        total = jnp.zeros((16, 2 * HEAD), jnp.float32)
        for i in range(OWN):
            c = b + 2 * i
            at = 2 * width + i * 2 * HEAD
            if c < 16:
                total = total + got[c * 16:(c + 1) * 16, at:at + 2 * HEAD].astype(jnp.float32)
        key_gradient[b * 16:(b + 1) * 16, :] = total[:, :HEAD].astype(jnp.bfloat16)
        value_gradient[b * 16:(b + 1) * 16, :] = total[:, HEAD:].astype(jnp.bfloat16)


def pack_kernel(queries, grads, keys, values, place, kv, qd_a, qd_b):
    rows, width = queries.shape
    half = width // 2
    marks = jnp.broadcast_to(place[...].astype(jnp.float32).reshape(1, BLOCK), (PLACE_ROWS, BLOCK)).astype(jnp.bfloat16)
    marks = jnp.concatenate([marks, marks], axis=1)
    for k in range(kv.shape[0]):
        cols = slice(k * HEAD, (k + 1) * HEAD)
        kv[k] = jnp.concatenate([jnp.concatenate([keys[:, cols], values[:, cols]], axis=1), marks], axis=0)
    first = lax.axis_index("kvh") == 0
    for array, at in ((queries, 0), (grads, half)):
        low, high = array[:, :half], array[:, half:]
        qd_a[:, at:at + half] = jnp.where(first, low, high)
        qd_b[:, at:at + half] = jnp.where(first, high, low)


def copy_kernel(x, y):
    y[...] = x[...]


def shards(query_heads, key_heads, pool_values, output_grad, lengths, placement):
    dp_count, ctx_count, kvh_count = (lax.axis_size(name) for name in AXES)
    bf16, f32 = jnp.bfloat16, jnp.float32

    def place_of(d, c, k):
        return (d * ctx_count + c) * kvh_count + k

    def moved(value, target):
        pairs = [
            (place_of(d, c, k), place_of(*target(d, c, k)))
            for d in range(dp_count)
            for c in range(ctx_count)
            for k in range(kvh_count)
        ]
        return lax.ppermute(value, AXES, pairs)

    def to_group(d, c, k):
        return (d + c) % dp_count, c, k

    def to_group_swapped(d, c, k):
        return (d + c) % dp_count, c, k ^ 1

    rows = key_heads.shape[0]
    half_cols = query_heads.shape[1] // 2
    smem = pl.BlockSpec(memory_space=pltpu.SMEM)
    vmem = pl.BlockSpec(memory_space=pltpu.VMEM)
    params = pltpu.CompilerParams(vmem_limit_bytes=48 * 1024 * 1024)
    kv, qd_a, qd_b = pl.pallas_call(
        pack_kernel,
        out_shape=(
            jax.ShapeDtypeStruct((kvh_count, rows + PLACE_ROWS, 2 * HEAD), bf16),
            jax.ShapeDtypeStruct((rows, 2 * half_cols), bf16),
            jax.ShapeDtypeStruct((rows, 2 * half_cols), bf16),
        ),
        in_specs=[vmem] * 5,
        out_specs=(vmem,) * 3,
        name="pack",
    )(query_heads, output_grad, key_heads, pool_values, placement)
    kv = moved(kv, to_group)
    held = pl.pallas_call(
        copy_kernel,
        out_shape=jax.ShapeDtypeStruct((16, HEAD), bf16),
        in_specs=[pl.BlockSpec(memory_space=pltpu.VMEM)],
        out_specs=pl.BlockSpec(memory_space=pltpu.VMEM),
        cost_estimate=pl.CostEstimate(flops=13800000000, bytes_accessed=300000, transcendentals=0),
        name="hold",
    )(kv[0, :16, :HEAD])
    kv, held = lax.optimization_barrier((kv, held))
    qd_a = moved(qd_a, to_group)
    qd_b = moved(qd_b, to_group_swapped)
    half_count = ctx_count // 2
    copies = jnp.broadcast_to(kv[None], (half_count,) + kv.shape)
    copies = copies.reshape((ctx_count,) + kv.shape[1:])
    parities = [
        [c * kvh_count + k for c in range(parity, ctx_count, 2) for k in range(kvh_count)] for parity in range(2)
    ]
    to_twin = [(c, c ^ 1) for c in range(ctx_count)]

    def gathered(copies):
        kv = lax.all_to_all(
            copies, ("ctx", "kvh"), split_axis=0, concat_axis=0, axis_index_groups=parities, tiled=True
        )
        return kv, lax.ppermute(kv, "ctx", to_twin)

    kv, kv_twin = lax.cond(lax.axis_index(AXES[0]) >= 0, gathered, lambda copies: (copies, copies), copies)

    def marks_of(a):
        return a.reshape((half_count, kvh_count) + a.shape[1:])[:, 0, rows, :BLOCK].astype(f32)

    place = jnp.concatenate([marks_of(kv), marks_of(kv_twin)], axis=0)
    keys = WINDOW * BLOCK
    sent, own_grad, twin_grad, box = pl.pallas_call(
        attention_kernel,
        out_shape=(
            jax.ShapeDtypeStruct((256, 2 * half_cols), bf16),
            jax.ShapeDtypeStruct((OWN * BLOCK, 2 * HEAD), f32),
            jax.ShapeDtypeStruct(((WINDOW - OWN) * BLOCK, 2 * HEAD), bf16),
            jax.ShapeDtypeStruct((ctx_count, BLOCK), f32),
        ),
        in_specs=[smem] + [vmem] * 5,
        out_specs=(vmem,) * 4,
        scratch_shapes=[
            pltpu.VMEM((keys, HEAD), bf16),
            pltpu.VMEM((keys, HEAD), bf16),
            pltpu.VMEM((half_cols, HEAD), bf16),
            pltpu.VMEM((half_cols, HEAD), bf16),
            pltpu.VMEM((keys, half_cols), bf16),
            pltpu.VMEM((keys, half_cols), bf16),
            pltpu.VMEM((keys, GROUP * HEAD), f32),
            pltpu.VMEM((keys, GROUP * HEAD), f32),
        ],
        compiler_params=params,
        name="attention",
    )(lengths.T, place, qd_a, qd_b, kv, kv_twin)
    twin_grad = lax.ppermute(twin_grad, "ctx", to_twin)
    sent = pl.pallas_call(
        slots_kernel,
        out_shape=jax.ShapeDtypeStruct((256, 2 * half_cols + OWN * 2 * HEAD), bf16),
        in_specs=[vmem] * 4,
        out_specs=vmem,
        compiler_params=params,
        name="slots",
    )(box, sent, own_grad, twin_grad)
    boxes = sent.reshape(ctx_count, 16, sent.shape[1])
    got = lax.all_to_all(boxes, "ctx", split_axis=0, concat_axis=0, tiled=True)
    return pl.pallas_call(
        landing_kernel,
        out_shape=(
            jax.ShapeDtypeStruct((256, half_cols), bf16),
            jax.ShapeDtypeStruct((256, half_cols), bf16),
            jax.ShapeDtypeStruct((256, HEAD), bf16),
            jax.ShapeDtypeStruct((256, HEAD), bf16),
        ),
        in_specs=[vmem],
        out_specs=(vmem,) * 4,
        compiler_params=params,
        name="landing",
    )(got.reshape(256, -1))


def solution(mesh):
    in_specs = (
        P(AXES, None),
        P(AXES, None),
        P(AXES, None),
        P(AXES, None),
        P(),
        P(("dp", "ctx")),
    )
    out_specs = (P(("dp", "ctx"), "kvh"),) * 4
    return jax.shard_map(shards, mesh=mesh, in_specs=in_specs, out_specs=out_specs, check_vma=False)
```

```python
import math

import jax
import jax.numpy as jnp
from jax import lax
from jax.experimental import pallas as pl
from jax.experimental.pallas import tpu as pltpu
from jax.sharding import PartitionSpec as P

HEAD = 128
BLOCK = 128
WINDOW = 9
CHUNK = 3
GROUP = 7
OWN = 5
PLACE_ROWS = 8
AXES = ("dp", "ctx", "kvh")
MASKED_LOGIT = -1e30


def dot_nt(a, b):
    return lax.dot_general(a, b, (((1,), (1,)), ((), ())), preferred_element_type=jnp.float32)


def dot_nn(a, b):
    return jnp.dot(a, b, preferred_element_type=jnp.float32)


def slots_of(place):
    lanes = lax.broadcasted_iota(jnp.int32, (BLOCK, BLOCK), 1)
    subs = lax.broadcasted_iota(jnp.int32, (BLOCK, BLOCK), 0)
    earlier = jnp.where(subs < lanes, 1.0, 0.0).astype(jnp.bfloat16)
    hits = [jnp.where(place == float(e), 1.0, 0.0) for e in range(16)]
    counts = dot_nn(jnp.concatenate(hits, axis=0).astype(jnp.bfloat16), earlier)
    slot = place * 16.0
    for e in range(16):
        slot = slot + hits[e] * counts[e * 16:(e + 1) * 16, :]
    return slot


def one_hot_slots(slot):
    slots = lax.broadcasted_iota(jnp.int32, (256, BLOCK), 0).astype(jnp.float32)
    return jnp.where(slot == slots, 1.0, 0.0).astype(jnp.bfloat16)


def attention_kernel(
    lengths, qd_a, qd_b, kv_own, kv_twin, rows_t, own_grad, twin_grad, box, k_all, s_all, v_all, q_all, g_all, w_all, logit, expo
):
    heads = qd_a.shape[1] // (2 * HEAD)
    width = heads * HEAD
    half_rows = BLOCK // 2
    scaling = 1.0 / math.sqrt(HEAD)
    exponent = scaling * math.log2(math.e)
    group, ctx_pos, kvh_pos = (lax.axis_index(name) for name in AXES)
    off = kvh_pos * half_rows
    begin1 = lengths[0, group]
    begin2 = begin1 + lengths[1, group]
    begin3 = begin2 + lengths[2, group]
    lane = lax.broadcasted_iota(jnp.int32, (1, BLOCK), 1)
    position = ctx_pos * BLOCK + (lane ^ off)
    start = jnp.where(
        position >= begin3,
        begin3,
        jnp.where(position >= begin2, begin2, jnp.where(position >= begin1, begin1, 0)),
    )
    first = (ctx_pos - (WINDOW - 1)) * BLOCK
    row = lax.broadcasted_iota(jnp.int32, (BLOCK, BLOCK), 0)
    for t in range(WINDOW):
        block = jnp.maximum(ctx_pos - (WINDOW - 1) + t, 0)
        kv = kv_own if t % 2 == 0 else kv_twin
        for part in range(2):
            rows = slice(t * BLOCK + part * half_rows, t * BLOCK + (part + 1) * half_rows)
            k_all[rows, :] = kv[2 * (block // 2) + part, 0:half_rows, 0:HEAD]
            v_all[rows, :] = kv[2 * (block // 2) + part, 0:half_rows, HEAD:2 * HEAD]
    marks = [
        kv[2 * j, :, 0:HEAD].astype(jnp.float32)[half_rows:half_rows + 1, :] for kv in (kv_own, kv_twin) for j in range(8)
    ]
    box[...] = slots_of(jnp.concatenate(marks, axis=0))
    value_t = v_all[...].T
    for h in range(heads):
        cols = slice(h * HEAD, (h + 1) * HEAD)
        gcols = slice(width + h * HEAD, width + (h + 1) * HEAD)
        q_all[cols, :] = jnp.concatenate([qd_a[:, cols], qd_b[:, cols]], axis=0)
        g_all[cols, :] = jnp.concatenate([qd_a[:, gcols], qd_b[:, gcols]], axis=0)

    def folded(x, op):
        x = x.reshape(x.shape[0] // 8, 8, x.shape[1])
        out = x[0]
        for i in range(1, x.shape[0]):
            out = op(out, x[i])
        return out

    span = CHUNK * BLOCK
    chunk_at = [slice(t * span, (t + 1) * span) for t in range(WINDOW // CHUNK)]
    wide = lax.broadcasted_iota(jnp.int32, (span, BLOCK), 0)
    for h in range(0, heads, GROUP):
        n = min(GROUP, heads - h)
        cols = slice(h * HEAD, (h + n) * HEAD)
        q, g = q_all[cols, :], g_all[cols, :]
        top = None
        for t, rows in enumerate(chunk_at):
            x = dot_nt(k_all[rows, :], q)
            base = first + t * span
            visible = wide >= start - base
            if t == len(chunk_at) - 1:
                visible = visible & (wide <= position - base)
            x = jnp.where(jnp.concatenate([visible] * n, axis=1), x, MASKED_LOGIT)
            logit[rows, cols] = x
            x = folded(x, jnp.maximum)
            top = x if top is None else jnp.maximum(top, x)
        top = jnp.max(top, axis=0, keepdims=True)
        total = None
        for t, rows in enumerate(chunk_at):
            x = jnp.exp2((logit[rows, cols] - top) * exponent)
            expo[rows, cols] = x
            x = folded(x, jnp.add)
            total = x if total is None else total + x
        inverse = 1.0 / jnp.sum(total, axis=0, keepdims=True)
        for t, rows in enumerate(chunk_at):
            w_all[rows, cols] = (expo[rows, cols] * inverse).astype(jnp.bfloat16)
        out_b = dot_nn(value_t, w_all[:, cols]).astype(jnp.bfloat16)
        rows_t[:, cols] = out_b
        g_t = g.astype(jnp.float32).T
        delta = jnp.sum(g_t * out_b.astype(jnp.float32), axis=0, keepdims=True)
        for t, rows in enumerate(chunk_at):
            dprob = dot_nt(v_all[rows, :], g)
            s_all[rows, cols] = ((expo[rows, cols] * inverse) * (dprob - delta)).astype(jnp.bfloat16)
    q_rows = q_all[...]
    g_rows = g_all[...]
    grad_k = dot_nn(s_all[...], q_rows) * scaling
    grad_v = dot_nn(w_all[...], g_rows)
    for t in range(WINDOW):
        rows = slice(t * BLOCK, (t + 1) * BLOCK)
        step = WINDOW - 1 - t
        out = twin_grad if step % 2 else own_grad
        at = slice(step // 2 * BLOCK, (step // 2 + 1) * BLOCK)
        out[at, :HEAD] = grad_k[rows, :].astype(out.dtype)
        out[at, HEAD:] = grad_v[rows, :].astype(out.dtype)


def row_slots_kernel(box, rows_t, k_all, s_all, sent):
    ctx_pos, kvh_pos = lax.axis_index(AXES[1]), lax.axis_index(AXES[2])
    half_rows = BLOCK // 2
    own = box[pl.ds(ctx_pos // 2, 1), :]
    own = jnp.where(kvh_pos == 0, own, jnp.concatenate([own[:, half_rows:], own[:, :half_rows]], axis=1))
    slots = one_hot_slots(own)
    grads_t = (dot_nn(k_all[...].T, s_all[...]) * (1.0 / math.sqrt(HEAD))).astype(jnp.bfloat16)
    count = rows_t.shape[1] // HEAD
    stacked = jnp.concatenate(
        [a[:, i * HEAD:(i + 1) * HEAD] for a in (rows_t[...], grads_t) for i in range(count)], axis=0
    )
    sent[:, :2 * rows_t.shape[1]] = dot_nt(slots, stacked).astype(jnp.bfloat16)


def grad_slots_kernel(box, begun, own_grad, twin_grad, sent):
    ctx_pos = lax.axis_index(AXES[1])
    odd = ctx_pos % 2 == 1
    width = sent.shape[1] - OWN * 2 * HEAD
    for i in range(OWN):
        total = own_grad[i * BLOCK:(i + 1) * BLOCK, :]
        zero = jnp.zeros(total.shape, jnp.float32)
        later = twin_grad[(i - 1) * BLOCK:i * BLOCK, :].astype(jnp.float32) if i > 0 else zero
        level = twin_grad[i * BLOCK:(i + 1) * BLOCK, :].astype(jnp.float32) if i < OWN - 1 else zero
        total = total + jnp.where(odd, later, level)
        block = jnp.maximum(ctx_pos - 2 * i, 0)
        hot = one_hot_slots(box[pl.ds(block // 2, 1), :])
        at = width + i * 2 * HEAD
        sent[:, at:at + 2 * HEAD] = dot_nn(hot, total.astype(jnp.bfloat16)).astype(jnp.bfloat16)


def landing_kernel(got, attended, grad_query, key_gradient, value_gradient):
    width = attended.shape[1]
    rows = got.shape[0]
    attended[...] = got[:, :width]
    grad_query[...] = got[:, width:2 * width]
    for b in range(16):
        total = jnp.zeros((16, 2 * HEAD), jnp.float32)
        for i in range(OWN):
            c = b + 2 * i
            at = 2 * width + i * 2 * HEAD
            if c < 16:
                total = total + got[c * 16:(c + 1) * 16, at:at + 2 * HEAD].astype(jnp.float32)
        key_gradient[b * 16:(b + 1) * 16, :] = total[:, :HEAD].astype(jnp.bfloat16)
        value_gradient[b * 16:(b + 1) * 16, :] = total[:, HEAD:].astype(jnp.bfloat16)


def pack_kernel(queries, grads, keys, values, place, kv, qd_a, qd_b):
    rows, width = queries.shape
    half = width // 2
    marks = jnp.broadcast_to(place[...].astype(jnp.float32).reshape(1, BLOCK), (PLACE_ROWS, BLOCK)).astype(jnp.bfloat16)
    marks = jnp.concatenate([marks, marks], axis=1)
    for k in range(kv.shape[0]):
        cols = slice(k * HEAD, (k + 1) * HEAD)
        kv[k] = jnp.concatenate([jnp.concatenate([keys[:, cols], values[:, cols]], axis=1), marks], axis=0)
    first = lax.axis_index("kvh") == 0
    for array, at in ((queries, 0), (grads, half)):
        low, high = array[:, :half], array[:, half:]
        qd_a[:, at:at + half] = jnp.where(first, low, high)
        qd_b[:, at:at + half] = jnp.where(first, high, low)


def copies_kernel(kv, copies):
    for i in range(copies.shape[0]):
        copies[i] = kv[i % kv.shape[0]]


def shards(query_heads, key_heads, pool_values, output_grad, lengths, placement):
    dp_count, ctx_count, kvh_count = (lax.axis_size(name) for name in AXES)
    bf16, f32 = jnp.bfloat16, jnp.float32

    def place_of(d, c, k):
        return (d * ctx_count + c) * kvh_count + k

    def moved(value, target):
        pairs = [
            (place_of(d, c, k), place_of(*target(d, c, k)))
            for d in range(dp_count)
            for c in range(ctx_count)
            for k in range(kvh_count)
        ]
        return lax.ppermute(value, AXES, pairs)

    def to_group(d, c, k):
        return (d + c) % dp_count, c, k

    def aside(d, c, k):
        return d, c ^ 4, k ^ 1

    def to_group_from_aside(d, c, k):
        return to_group(d, c ^ 4, k)

    rows = key_heads.shape[0]
    half_cols = query_heads.shape[1] // 2
    smem = pl.BlockSpec(memory_space=pltpu.SMEM)
    vmem = pl.BlockSpec(memory_space=pltpu.VMEM)
    params = pltpu.CompilerParams(vmem_limit_bytes=48 * 1024 * 1024)
    kv, qd_a, qd_b = pl.pallas_call(
        pack_kernel,
        out_shape=(
            pltpu.VMEM((kvh_count, rows + PLACE_ROWS, 2 * HEAD), bf16),
            pltpu.VMEM((rows, 2 * half_cols), bf16),
            pltpu.VMEM((rows, 2 * half_cols), bf16),
        ),
        in_specs=[vmem] * 5,
        out_specs=(vmem,) * 3,
        name="pack",
    )(query_heads, output_grad, key_heads, pool_values, placement)
    kv = moved(kv, to_group)
    qd_a = moved(qd_a, to_group)
    qd_b = moved(moved(qd_b, aside), to_group_from_aside)
    copies = pl.pallas_call(
        copies_kernel,
        out_shape=jax.ShapeDtypeStruct((ctx_count,) + kv.shape[1:], bf16),
        in_specs=[vmem],
        out_specs=vmem,
        cost_estimate=pl.CostEstimate(flops=13800000000, bytes_accessed=300000, transcendentals=0),
        compiler_params=params,
        name="copies",
    )(kv)
    parities = [
        [c * kvh_count + k for c in range(parity, ctx_count, 2) for k in range(kvh_count)] for parity in range(2)
    ]
    to_twin = [(c, c ^ 1) for c in range(ctx_count)]

    def gathered(copies):
        kv = lax.all_to_all(
            copies, ("ctx", "kvh"), split_axis=0, concat_axis=0, axis_index_groups=parities, tiled=True
        )
        return kv, lax.ppermute(kv, "ctx", to_twin)

    kv, kv_twin = lax.cond(lax.axis_index(AXES[0]) >= 0, gathered, lambda copies: (copies, copies), copies)

    keys = WINDOW * BLOCK
    rows_t, own_grad, twin_grad, box, k_all, s_all = pl.pallas_call(
        attention_kernel,
        out_shape=(
            pltpu.VMEM((HEAD, half_cols), bf16),
            pltpu.VMEM((OWN * BLOCK, 2 * HEAD), f32),
            pltpu.VMEM(((WINDOW - OWN) * BLOCK, 2 * HEAD), bf16),
            pltpu.VMEM((ctx_count, BLOCK), f32),
            pltpu.VMEM((keys, HEAD), bf16),
            pltpu.VMEM((keys, half_cols), bf16),
        ),
        in_specs=[smem] + [vmem] * 4,
        out_specs=(vmem,) * 6,
        scratch_shapes=[
            pltpu.VMEM((keys, HEAD), bf16),
            pltpu.VMEM((half_cols, HEAD), bf16),
            pltpu.VMEM((half_cols, HEAD), bf16),
            pltpu.VMEM((keys, half_cols), bf16),
            pltpu.VMEM((keys, 7 * HEAD), f32),
            pltpu.VMEM((keys, 7 * HEAD), f32),
        ],
        compiler_params=params,
        name="attention",
    )(lengths.T, qd_a, qd_b, kv, kv_twin)
    twin_grad = lax.ppermute(twin_grad, "ctx", to_twin)
    sent_shape = jax.ShapeDtypeStruct((256, 2 * half_cols + OWN * 2 * HEAD), bf16)
    sent = pl.pallas_call(
        row_slots_kernel,
        out_shape=sent_shape,
        in_specs=[vmem] * 4,
        out_specs=vmem,
        compiler_params=params,
        name="row_slots",
    )(box, rows_t, k_all, s_all)
    sent = pl.pallas_call(
        grad_slots_kernel,
        out_shape=sent_shape,
        in_specs=[vmem, pl.BlockSpec(memory_space=pl.ANY), vmem, vmem],
        out_specs=vmem,
        input_output_aliases={1: 0},
        compiler_params=params,
        name="grad_slots",
    )(box, sent, own_grad, twin_grad)
    boxes = sent.reshape(ctx_count, 16, sent.shape[1])
    got = lax.all_to_all(boxes, "ctx", split_axis=0, concat_axis=0, tiled=True)
    return pl.pallas_call(
        landing_kernel,
        out_shape=(
            jax.ShapeDtypeStruct((256, half_cols), bf16),
            jax.ShapeDtypeStruct((256, half_cols), bf16),
            jax.ShapeDtypeStruct((256, HEAD), bf16),
            jax.ShapeDtypeStruct((256, HEAD), bf16),
        ),
        in_specs=[vmem],
        out_specs=(vmem,) * 4,
        compiler_params=params,
        name="landing",
    )(got.reshape(256, -1))


def solution(mesh):
    in_specs = (
        P(AXES, None),
        P(AXES, None),
        P(AXES, None),
        P(AXES, None),
        P(),
        P(("dp", "ctx")),
    )
    out_specs = (P(("dp", "ctx"), "kvh"),) * 4
    return jax.shard_map(shards, mesh=mesh, in_specs=in_specs, out_specs=out_specs, check_vma=False)
```

```python
import math

import jax
import jax.numpy as jnp
from jax import lax
from jax.experimental import pallas as pl
from jax.experimental.pallas import tpu as pltpu
from jax.sharding import PartitionSpec as P

HEAD = 128
BLOCK = 128
WINDOW = 9
CHUNK = 3
GROUP = 7
OWN = 5
PLACE_ROWS = 8
AXES = ("dp", "ctx", "kvh")
MASKED_LOGIT = -1e30


def dot_nt(a, b):
    return lax.dot_general(a, b, (((1,), (1,)), ((), ())), preferred_element_type=jnp.float32)


def dot_nn(a, b):
    return jnp.dot(a, b, preferred_element_type=jnp.float32)


def slots_of(place):
    lanes = lax.broadcasted_iota(jnp.int32, (BLOCK, BLOCK), 1)
    subs = lax.broadcasted_iota(jnp.int32, (BLOCK, BLOCK), 0)
    earlier = jnp.where(subs < lanes, 1.0, 0.0).astype(jnp.bfloat16)
    hits = [jnp.where(place == float(e), 1.0, 0.0) for e in range(16)]
    counts = dot_nn(jnp.concatenate(hits, axis=0).astype(jnp.bfloat16), earlier)
    slot = place * 16.0
    blocks = place.shape[0]
    for e in range(16):
        slot = slot + hits[e] * counts[e * blocks:(e + 1) * blocks, :]
    return slot


def one_hot_slots(slot):
    slots = lax.broadcasted_iota(jnp.int32, (256, BLOCK), 0).astype(jnp.float32)
    return jnp.where(slot == slots, 1.0, 0.0).astype(jnp.bfloat16)


def attention_kernel(
    lengths, qd_a, qd_b, kv_own, kv_twin, rows_t, own_grad, twin_grad, box, k_all, s_all, v_all, q_all, g_all, w_all, logit, expo
):
    heads = qd_a.shape[1] // (2 * HEAD)
    width = heads * HEAD
    half_rows = BLOCK // 2
    scaling = 1.0 / math.sqrt(HEAD)
    exponent = scaling * math.log2(math.e)
    group, ctx_pos, kvh_pos = (lax.axis_index(name) for name in AXES)
    off = kvh_pos * half_rows
    begin1 = lengths[0, group]
    begin2 = begin1 + lengths[1, group]
    begin3 = begin2 + lengths[2, group]
    lane = lax.broadcasted_iota(jnp.int32, (1, BLOCK), 1)
    position = ctx_pos * BLOCK + (lane ^ off)
    start = jnp.where(
        position >= begin3,
        begin3,
        jnp.where(position >= begin2, begin2, jnp.where(position >= begin1, begin1, 0)),
    )
    first = (ctx_pos - (WINDOW - 1)) * BLOCK
    row = lax.broadcasted_iota(jnp.int32, (BLOCK, BLOCK), 0)
    for t in range(WINDOW):
        block = jnp.maximum(ctx_pos - (WINDOW - 1) + t, 0)
        kv = kv_own if t % 2 == 0 else kv_twin
        for part in range(2):
            rows = slice(t * BLOCK + part * half_rows, t * BLOCK + (part + 1) * half_rows)
            k_all[rows, :] = kv[2 * (block // 2) + part, 0:half_rows, 0:HEAD]
            v_all[rows, :] = kv[2 * (block // 2) + part, 0:half_rows, HEAD:2 * HEAD]
    marks = [
        kv[2 * j, :, 0:HEAD].astype(jnp.float32)[half_rows:half_rows + 1, :] for kv in (kv_own,) for j in range(8)
    ]
    box[...] = slots_of(jnp.concatenate(marks, axis=0))
    value_t = v_all[...].T
    for h in range(heads):
        cols = slice(h * HEAD, (h + 1) * HEAD)
        gcols = slice(width + h * HEAD, width + (h + 1) * HEAD)
        q_all[cols, :] = jnp.concatenate([qd_a[:, cols], qd_b[:, cols]], axis=0)
        g_all[cols, :] = jnp.concatenate([qd_a[:, gcols], qd_b[:, gcols]], axis=0)

    def folded(x, op):
        x = x.reshape(x.shape[0] // 8, 8, x.shape[1])
        out = x[0]
        for i in range(1, x.shape[0]):
            out = op(out, x[i])
        return out

    span = CHUNK * BLOCK
    chunk_at = [slice(t * span, (t + 1) * span) for t in range(WINDOW // CHUNK)]
    wide = lax.broadcasted_iota(jnp.int32, (span, BLOCK), 0)
    for h in range(0, heads, GROUP):
        n = min(GROUP, heads - h)
        cols = slice(h * HEAD, (h + n) * HEAD)
        q, g = q_all[cols, :], g_all[cols, :]
        top = None
        for t, rows in enumerate(chunk_at):
            x = dot_nt(k_all[rows, :], q)
            base = first + t * span
            visible = wide >= start - base
            if t == len(chunk_at) - 1:
                visible = visible & (wide <= position - base)
            x = jnp.where(jnp.concatenate([visible] * n, axis=1), x, MASKED_LOGIT)
            logit[rows, cols] = x
            x = folded(x, jnp.maximum)
            top = x if top is None else jnp.maximum(top, x)
        top = jnp.max(top, axis=0, keepdims=True)
        total = None
        for t, rows in enumerate(chunk_at):
            x = jnp.exp2((logit[rows, cols] - top) * exponent)
            expo[rows, cols] = x
            x = folded(x, jnp.add)
            total = x if total is None else total + x
        inverse = 1.0 / jnp.sum(total, axis=0, keepdims=True)
        for t, rows in enumerate(chunk_at):
            w_all[rows, cols] = (expo[rows, cols] * inverse).astype(jnp.bfloat16)
        out_b = dot_nn(value_t, w_all[:, cols]).astype(jnp.bfloat16)
        rows_t[:, cols] = out_b
        g_t = g.astype(jnp.float32).T
        delta = jnp.sum(g_t * out_b.astype(jnp.float32), axis=0, keepdims=True)
        for t, rows in enumerate(chunk_at):
            dprob = dot_nt(v_all[rows, :], g)
            s_all[rows, cols] = ((expo[rows, cols] * inverse) * (dprob - delta)).astype(jnp.bfloat16)
    q_rows = q_all[...]
    g_rows = g_all[...]
    grad_k = dot_nn(s_all[...], q_rows) * scaling
    grad_v = dot_nn(w_all[...], g_rows)
    for t in range(WINDOW):
        rows = slice(t * BLOCK, (t + 1) * BLOCK)
        step = WINDOW - 1 - t
        out = twin_grad if step % 2 else own_grad
        at = slice(step // 2 * BLOCK, (step // 2 + 1) * BLOCK)
        out[at, :HEAD] = grad_k[rows, :].astype(out.dtype)
        out[at, HEAD:] = grad_v[rows, :].astype(out.dtype)


def row_slots_kernel(box, rows_t, k_all, s_all, sent):
    ctx_pos, kvh_pos = lax.axis_index(AXES[1]), lax.axis_index(AXES[2])
    half_rows = BLOCK // 2
    own = box[pl.ds(ctx_pos // 2, 1), :]
    own = jnp.where(kvh_pos == 0, own, jnp.concatenate([own[:, half_rows:], own[:, :half_rows]], axis=1))
    slots = one_hot_slots(own)
    grads_t = (dot_nn(k_all[...].T, s_all[...]) * (1.0 / math.sqrt(HEAD))).astype(jnp.bfloat16)
    count = rows_t.shape[1] // HEAD
    stacked = jnp.concatenate(
        [a[:, i * HEAD:(i + 1) * HEAD] for a in (rows_t[...], grads_t) for i in range(count)], axis=0
    )
    sent[:, :2 * rows_t.shape[1]] = dot_nt(slots, stacked).astype(jnp.bfloat16)


def grad_slots_kernel(box, begun, own_grad, twin_grad, sent):
    ctx_pos = lax.axis_index(AXES[1])
    odd = ctx_pos % 2 == 1
    width = sent.shape[1] - OWN * 2 * HEAD
    for i in range(OWN):
        total = own_grad[i * BLOCK:(i + 1) * BLOCK, :]
        zero = jnp.zeros(total.shape, jnp.float32)
        later = twin_grad[(i - 1) * BLOCK:i * BLOCK, :].astype(jnp.float32) if i > 0 else zero
        level = twin_grad[i * BLOCK:(i + 1) * BLOCK, :].astype(jnp.float32) if i < OWN - 1 else zero
        total = total + jnp.where(odd, later, level)
        block = jnp.maximum(ctx_pos - 2 * i, 0)
        hot = one_hot_slots(box[pl.ds(block // 2, 1), :])
        at = width + i * 2 * HEAD
        sent[:, at:at + 2 * HEAD] = dot_nn(hot, total.astype(jnp.bfloat16)).astype(jnp.bfloat16)


def landing_kernel(got, attended, grad_query, key_gradient, value_gradient):
    width = attended.shape[1]
    rows = got.shape[0]
    attended[...] = got[:, :width]
    grad_query[...] = got[:, width:2 * width]
    for b in range(16):
        total = jnp.zeros((16, 2 * HEAD), jnp.float32)
        for i in range(OWN):
            c = b + 2 * i
            at = 2 * width + i * 2 * HEAD
            if c < 16:
                total = total + got[c * 16:(c + 1) * 16, at:at + 2 * HEAD].astype(jnp.float32)
        key_gradient[b * 16:(b + 1) * 16, :] = total[:, :HEAD].astype(jnp.bfloat16)
        value_gradient[b * 16:(b + 1) * 16, :] = total[:, HEAD:].astype(jnp.bfloat16)


def pack_kernel(queries, grads, keys, values, place, kv, qd_a, qd_b):
    rows, width = queries.shape
    half = width // 2
    marks = jnp.broadcast_to(place[...].astype(jnp.float32).reshape(1, BLOCK), (PLACE_ROWS, BLOCK)).astype(jnp.bfloat16)
    marks = jnp.concatenate([marks, marks], axis=1)
    for k in range(kv.shape[0]):
        cols = slice(k * HEAD, (k + 1) * HEAD)
        kv[k] = jnp.concatenate([jnp.concatenate([keys[:, cols], values[:, cols]], axis=1), marks], axis=0)
    first = lax.axis_index("kvh") == 0
    for array, at in ((queries, 0), (grads, half)):
        low, high = array[:, :half], array[:, half:]
        qd_a[:, at:at + half] = jnp.where(first, low, high)
        qd_b[:, at:at + half] = jnp.where(first, high, low)


def copies_kernel(kv, copies):
    for i in range(copies.shape[0]):
        copies[i] = kv[i % kv.shape[0]]


def shards(query_heads, key_heads, pool_values, output_grad, lengths, placement):
    dp_count, ctx_count, kvh_count = (lax.axis_size(name) for name in AXES)
    bf16, f32 = jnp.bfloat16, jnp.float32

    def place_of(d, c, k):
        return (d * ctx_count + c) * kvh_count + k

    def moved(value, target):
        pairs = [
            (place_of(d, c, k), place_of(*target(d, c, k)))
            for d in range(dp_count)
            for c in range(ctx_count)
            for k in range(kvh_count)
        ]
        return lax.ppermute(value, AXES, pairs)

    def to_group(d, c, k):
        return (d + c) % dp_count, c, k

    def aside(d, c, k):
        return d, c ^ 4, k ^ 1

    def to_group_from_aside(d, c, k):
        return to_group(d, c ^ 4, k)

    rows = key_heads.shape[0]
    half_cols = query_heads.shape[1] // 2
    smem = pl.BlockSpec(memory_space=pltpu.SMEM)
    vmem = pl.BlockSpec(memory_space=pltpu.VMEM)
    params = pltpu.CompilerParams(vmem_limit_bytes=48 * 1024 * 1024)
    kv, qd_a, qd_b = pl.pallas_call(
        pack_kernel,
        out_shape=(
            pltpu.VMEM((kvh_count, rows + PLACE_ROWS, 2 * HEAD), bf16),
            pltpu.VMEM((rows, 2 * half_cols), bf16),
            pltpu.VMEM((rows, 2 * half_cols), bf16),
        ),
        in_specs=[vmem] * 5,
        out_specs=(vmem,) * 3,
        name="pack",
    )(query_heads, output_grad, key_heads, pool_values, placement)
    kv = moved(kv, to_group)
    qd_a = moved(qd_a, to_group)
    qd_b = moved(moved(qd_b, aside), to_group_from_aside)
    copies = pl.pallas_call(
        copies_kernel,
        out_shape=jax.ShapeDtypeStruct((ctx_count,) + kv.shape[1:], bf16),
        in_specs=[vmem],
        out_specs=vmem,
        cost_estimate=pl.CostEstimate(flops=13800000000, bytes_accessed=300000, transcendentals=0),
        compiler_params=params,
        name="copies",
    )(kv)
    parities = [
        [c * kvh_count + k for c in range(parity, ctx_count, 2) for k in range(kvh_count)] for parity in range(2)
    ]
    to_twin = [(c, c ^ 1) for c in range(ctx_count)]

    def gathered(copies):
        kv = lax.all_to_all(
            copies, ("ctx", "kvh"), split_axis=0, concat_axis=0, axis_index_groups=parities, tiled=True
        )
        return kv, lax.ppermute(kv, "ctx", to_twin)

    kv, kv_twin = lax.cond(lax.axis_index(AXES[0]) >= 0, gathered, lambda copies: (copies, copies), copies)

    keys = WINDOW * BLOCK
    rows_t, own_grad, twin_grad, box, k_all, s_all = pl.pallas_call(
        attention_kernel,
        out_shape=(
            pltpu.VMEM((HEAD, half_cols), bf16),
            pltpu.VMEM((OWN * BLOCK, 2 * HEAD), f32),
            pltpu.VMEM(((WINDOW - OWN) * BLOCK, 2 * HEAD), bf16),
            pltpu.VMEM((ctx_count // 2, BLOCK), f32),
            pltpu.VMEM((keys, HEAD), bf16),
            pltpu.VMEM((keys, half_cols), bf16),
        ),
        in_specs=[smem] + [vmem] * 4,
        out_specs=(vmem,) * 6,
        scratch_shapes=[
            pltpu.VMEM((keys, HEAD), bf16),
            pltpu.VMEM((half_cols, HEAD), bf16),
            pltpu.VMEM((half_cols, HEAD), bf16),
            pltpu.VMEM((keys, half_cols), bf16),
            pltpu.VMEM((keys, 7 * HEAD), f32),
            pltpu.VMEM((keys, 7 * HEAD), f32),
        ],
        compiler_params=params,
        name="attention",
    )(lengths.T, qd_a, qd_b, kv, kv_twin)
    twin_grad = lax.ppermute(twin_grad, "ctx", to_twin)
    sent_shape = jax.ShapeDtypeStruct((256, 2 * half_cols + OWN * 2 * HEAD), bf16)
    sent = pl.pallas_call(
        row_slots_kernel,
        out_shape=sent_shape,
        in_specs=[vmem] * 4,
        out_specs=vmem,
        compiler_params=params,
        name="row_slots",
    )(box, rows_t, k_all, s_all)
    sent = pl.pallas_call(
        grad_slots_kernel,
        out_shape=sent_shape,
        in_specs=[vmem, pl.BlockSpec(memory_space=pl.ANY), vmem, vmem],
        out_specs=vmem,
        input_output_aliases={1: 0},
        compiler_params=params,
        name="grad_slots",
    )(box, sent, own_grad, twin_grad)
    boxes = sent.reshape(ctx_count, 16, sent.shape[1])
    got = lax.all_to_all(boxes, "ctx", split_axis=0, concat_axis=0, tiled=True)
    return pl.pallas_call(
        landing_kernel,
        out_shape=(
            jax.ShapeDtypeStruct((256, half_cols), bf16),
            jax.ShapeDtypeStruct((256, half_cols), bf16),
            jax.ShapeDtypeStruct((256, HEAD), bf16),
            jax.ShapeDtypeStruct((256, HEAD), bf16),
        ),
        in_specs=[vmem],
        out_specs=(vmem,) * 4,
        compiler_params=params,
        name="landing",
    )(got.reshape(256, -1))


def solution(mesh):
    in_specs = (
        P(AXES, None),
        P(AXES, None),
        P(AXES, None),
        P(AXES, None),
        P(),
        P(("dp", "ctx")),
    )
    out_specs = (P(("dp", "ctx"), "kvh"),) * 4
    return jax.shard_map(shards, mesh=mesh, in_specs=in_specs, out_specs=out_specs, check_vma=False)
```
